32 devices in a mesh: wave: 16 (over z, x, core), lev: 2 (over y).
Axes of the slice: x: 2, y: 2, z: 4, core: 2. Of those that a mesh axis runs over, the one named last changes fastest.
Arguments:
- control: bfloat16 [1536, 1536, 2, 137], P(('wave', 'lev')), may hold values from -6 to 6
- covariance: bfloat16 [1536, 64, 137], P(('wave', 'lev')), may hold values from -0.013671875 to 0.013671875
- legendre: bfloat16 [1536, 1536, 16], P(('wave', 'lev')), may hold values from -0.21875 to 0.21875
- wave_order: int32 [1536], replicated, may hold values from 0 to 1535, each once
- lat_order: int32 [32], replicated, may hold values from 0 to 31, each once
- cycle_points: int32 [16], replicated, may hold values from 2048 to 6160, as said below
Outputs:
- grid: bfloat16 [32, 64, 2048], P(('wave', 'lev'))
The draws below stay inside these ranges and needn't reach their ends.
Inputs may be any that keep to these rules, and one draw needn't show every extreme that they name: cycle_points[i] is a multiple of 4, and at least 2048.
All inputs are finite; a program needn't handle non-finite values.
Results may differ from the reference program's by a relative error of at most 0.0062.
Values may be sent and summed in bfloat16 or wider, within the bound.
A program may use at most 192 MiB of HBM per device.

```python
import jax
import jax.numpy as jnp
from jax import lax

M = 1536
LEVELS = 137
SLAB = 64
LONW = 2048
LAT = 32
LATH = 16


def draw_cycle_points(key, part):
    key = jax.random.fold_in(key, 7)
    first_key, second_key = jax.random.split(key)
    cycles = jax.random.randint(first_key, (LATH,), LONW // 4, M + 5)
    marked = jax.random.randint(second_key, (), 0, LATH)
    cycles = jnp.where(jnp.arange(LATH) == marked, M + 4, cycles)
    return (4 * cycles).astype(jnp.int32)


def level_of(stream_key, extent, cuts, low, largest):
    gain = 1.0
    for axis_at, blocks in cuts:
        draws = jax.random.uniform(jax.random.fold_in(jax.random.fold_in(stream_key, 6), axis_at), (blocks,), jnp.float32, low / len(cuts), largest / len(cuts))
        gain = gain * jnp.repeat(jnp.exp(draws), extent[axis_at] // blocks).reshape((-1,) + (1,) * (len(extent) - 1 - axis_at))
    return gain


def scatter_about(stream_key, shape, deviation, bound, cuts=(), kind=jnp.bfloat16):
    array = jax.random.normal(stream_key, shape, jnp.float32) * deviation
    if len(cuts) > 0:
        array = level_of(stream_key, shape, cuts, -0.22, 0.18) * array
    return jnp.clip(array, min=-bound, max=bound).astype(kind)


def setup_inputs(seed: int = 0) -> dict:
    key_of = jax.random.split(jax.random.key(seed), 7)
    return {
        "control": scatter_about(key_of[0], (M, M, 2, LEVELS), 1.0, 6.0, ((0, 32),)),
        "covariance": scatter_about(key_of[1], (M, SLAB, LEVELS), (LEVELS * M) ** -0.5, 0.013671875, ((0, 32),)),
        "legendre": scatter_about(key_of[2], (M, M, LATH), (M // 2) ** -0.5, 0.21875, ((0, 32),)),
        "wave_order": jax.random.permutation(key_of[3], M).astype(jnp.int32),
        "lat_order": jax.random.permutation(key_of[4], LAT).astype(jnp.int32),
        "cycle_points": draw_cycle_points(jax.random.fold_in(key_of[6], 71), 0),
    }


def trig_tables(orders, points, factor, width):
    coarse = jnp.arange(width // 64, dtype=jnp.int32) * 64
    fine = jnp.arange(64, dtype=jnp.int32)
    scale = (2.0 * jnp.pi) / points.astype(jnp.float32)
    coarse_angle = ((orders[:, None] * coarse[None, :]) % points).astype(jnp.float32) * scale
    fine_angle = ((orders[:, None] * fine[None, :]) % points).astype(jnp.float32) * scale
    cos_c = jnp.cos(coarse_angle)[:, :, None]
    sin_c = jnp.sin(coarse_angle)[:, :, None]
    cos_f = jnp.cos(fine_angle)[:, None, :]
    sin_f = jnp.sin(fine_angle)[:, None, :]
    cosine = (cos_c * cos_f - sin_c * sin_f).reshape(orders.shape[0], width)
    sine = (sin_c * cos_f + cos_c * sin_f).reshape(orders.shape[0], width)
    cos_part = (factor[:, None] * cosine).astype(jnp.bfloat16)
    sin_part = (-factor[:, None] * sine).astype(jnp.bfloat16)
    return cos_part, sin_part


def reference(control, covariance, legendre, wave_order, lat_order, cycle_points):
    block_rows = 64
    total_ids = jnp.arange(M, dtype=jnp.int32)
    starts = jnp.arange(0, M, block_rows, dtype=jnp.int32)

    def slab_block(start):
        part_control = lax.dynamic_slice_in_dim(control, start, block_rows, 0).astype(jnp.float32)
        part_cov = lax.dynamic_slice_in_dim(covariance, start, block_rows, 0).astype(jnp.float32)
        produced = jnp.einsum('nrcl,nsl->nrcs', part_control, part_cov)
        totals = start + jnp.arange(block_rows, dtype=jnp.int32)
        usable = totals[:, None] >= wave_order[None, :]
        imag_usable = usable & (wave_order > 0)[None, :]
        weights = jnp.stack([usable, imag_usable], axis=2).astype(jnp.float32)
        return (produced * weights[:, :, :, None]).astype(jnp.bfloat16)

    slab = lax.map(slab_block, starts).reshape(M, M, 2, SLAB)

    def legendre_block(start):
        table = lax.dynamic_slice_in_dim(legendre, start, block_rows, 0).astype(jnp.float32)
        part = lax.dynamic_slice_in_dim(slab, start, block_rows, 1).astype(jnp.float32)
        orders = lax.dynamic_slice_in_dim(wave_order, start, block_rows, 0)
        parity = (total_ids[None, :] + orders[:, None]) % 2
        even_table = table * (parity == 0).astype(jnp.float32)[:, :, None]
        odd_table = table * (parity == 1).astype(jnp.float32)[:, :, None]
        even_sum = jnp.einsum('rnk,nrcs->rkcs', even_table, part)
        odd_sum = jnp.einsum('rnk,nrcs->rkcs', odd_table, part)
        return jnp.concatenate([even_sum + odd_sum, even_sum - odd_sum], axis=1).astype(jnp.bfloat16)

    coeffs = lax.map(legendre_block, starts).reshape(M, LAT, 2, SLAB)

    factor = jnp.where(wave_order == 0, 1.0, 2.0).astype(jnp.float32)

    def grid_row(latitude):
        points = cycle_points[latitude % LATH]
        cos_part, sin_part = trig_tables(wave_order, points, factor, LONW)
        picked = lax.dynamic_index_in_dim(coeffs, latitude, 1, keepdims=False)
        result = jnp.dot(picked[:, 0, :].T, cos_part, preferred_element_type=jnp.float32)
        result = result + jnp.dot(picked[:, 1, :].T, sin_part, preferred_element_type=jnp.float32)
        return result.astype(jnp.bfloat16)

    return lax.map(grid_row, lat_order)
```

```python
import functools

import jax
import jax.numpy as jnp
from jax import lax
from jax.experimental import pallas as pl
from jax.experimental.pallas import tpu as pltpu
from jax.sharding import PartitionSpec as P

LONW = 2048


def trig_tables(orders, points, factor, width):
    coarse = jnp.arange(width // 64, dtype=jnp.int32) * 64
    fine = jnp.arange(64, dtype=jnp.int32)
    scale = 2.0 * jnp.pi / points.astype(jnp.float32)
    coarse_angle = (orders[:, None] * coarse[None, :] % points).astype(jnp.float32) * scale
    fine_angle = (orders[:, None] * fine[None, :] % points).astype(jnp.float32) * scale
    cos_c = jnp.cos(coarse_angle)[:, :, None]
    sin_c = jnp.sin(coarse_angle)[:, :, None]
    cos_f = jnp.cos(fine_angle)[:, None, :]
    sin_f = jnp.sin(fine_angle)[:, None, :]
    cosine = (cos_c * cos_f - sin_c * sin_f).reshape(orders.shape[0], width)
    sine = (sin_c * cos_f + cos_c * sin_f).reshape(orders.shape[0], width)
    cos_part = (factor[:, None] * cosine).astype(jnp.bfloat16)
    sin_part = (-factor[:, None] * sine).astype(jnp.bfloat16)
    return (cos_part, sin_part)


def exchange_slab(control, covariance, legendre, wave_order, lat_order, cycle_points):
    wave_count = lax.axis_size("wave")
    level_count = lax.axis_size("lev")
    own_totals = control.shape[0]
    total = control.shape[1]
    own_rows = legendre.shape[0]
    half_lats = legendre.shape[2]
    all_lats = lat_order.shape[0]
    own_lats = all_lats // (wave_count * level_count)
    flat_index = lax.axis_index(("wave", "lev"))
    total_ids = flat_index * own_totals + jnp.arange(own_totals, dtype=jnp.int32)
    usable = total_ids[:, None] >= wave_order[None, :]
    imag_usable = usable & (wave_order > 0)[None, :]
    weights = jnp.stack([usable, imag_usable], axis=2).astype(jnp.float32)
    produced = jnp.einsum("nrcl,nsl->nrcs", control, covariance, preferred_element_type=jnp.float32)
    slab = (produced * weights[:, :, :, None]).astype(jnp.bfloat16)
    slab_levels = slab.shape[3]
    moved = lax.all_to_all(
        lax.all_to_all(slab, "wave", split_axis=1, concat_axis=0, tiled=True),
        "lev",
        split_axis=1,
        concat_axis=0,
        tiled=True,
    )
    moved = moved.reshape(level_count, wave_count, own_totals, own_rows, 2, slab_levels)
    moved = jnp.transpose(moved, (1, 0, 2, 3, 4, 5)).reshape(total, own_rows, 2, slab_levels)
    own_orders = lax.dynamic_slice_in_dim(wave_order, flat_index * own_rows, own_rows, 0)
    odd_order = own_orders % 2 == 1
    paired = moved.reshape(total // 2, 2, own_rows, 2, slab_levels)
    pick_moved = odd_order[None, :, None, None]
    even_moved = jnp.where(pick_moved, paired[:, 1], paired[:, 0])
    odd_moved = jnp.where(pick_moved, paired[:, 0], paired[:, 1])
    table_pairs = legendre.reshape(own_rows, total // 2, 2, half_lats)
    pick_table = odd_order[:, None, None]
    even_table = jnp.where(pick_table, table_pairs[:, :, 1], table_pairs[:, :, 0])
    odd_table = jnp.where(pick_table, table_pairs[:, :, 0], table_pairs[:, :, 1])
    even_sum = jnp.einsum(
        "rqk,qrcs->rkcs", even_table, even_moved, preferred_element_type=jnp.float32
    )
    odd_sum = jnp.einsum("rqk,qrcs->rkcs", odd_table, odd_moved, preferred_element_type=jnp.float32)
    coeffs = jnp.concatenate([even_sum + odd_sum, even_sum - odd_sum], axis=1).astype(jnp.bfloat16)
    ordered = jnp.take(coeffs, lat_order, axis=1)
    arrived = lax.all_to_all(
        lax.all_to_all(ordered, "wave", split_axis=1, concat_axis=0, tiled=True),
        "lev",
        split_axis=1,
        concat_axis=0,
        tiled=True,
    )
    wave_list = (
        wave_order.reshape(wave_count, level_count, own_rows).transpose(1, 0, 2).reshape(total)
    )
    row_ids = flat_index * own_lats + jnp.arange(own_lats, dtype=jnp.int32)
    latitudes = jnp.take(lat_order, row_ids)
    by_latitude = jnp.moveaxis(arrived, 1, 0)
    factor = jnp.where(wave_list == 0, 1.0, 2.0).astype(jnp.float32)

    def grid_row(pieces):
        picked, latitude = pieces
        points = jnp.take(cycle_points, latitude % half_lats)
        cos_part, sin_part = trig_tables(wave_list, points, factor, LONW)
        trig_table = jnp.concatenate([cos_part, sin_part], axis=0)
        stacked = jnp.concatenate([picked[:, 0, :], picked[:, 1, :]], axis=0)
        result = jnp.einsum("ks,kj->sj", stacked, trig_table, preferred_element_type=jnp.float32)
        return result.astype(jnp.bfloat16)

    return lax.map(grid_row, (by_latitude, latitudes))


GROUP = 8
BLOCK = 128


def partial_kernel(lat_ref, slab_ref, table_ref, mask_ref, out_ref, turned, signed):
    totals, pairs, block = slab_ref.shape
    half = table_ref.shape[1]
    lats = out_ref.shape[0]
    depth = totals * GROUP

    def turn(n, carry):
        flipped = slab_ref[n].astype(jnp.float32).T
        start = pl.multiple_of(n * GROUP, GROUP)
        turned[:, pl.ds(start, GROUP), :] = flipped.reshape(block // GROUP, GROUP, pairs)
        return carry

    lax.fori_loop(0, totals, turn, 0, unroll=2)
    same = lax.broadcasted_iota(jnp.int32, (GROUP, depth), 1) % GROUP == lax.broadcasted_iota(
        jnp.int32, (GROUP, depth), 0
    )

    def group_sum(g):
        table = table_ref[g].astype(jnp.float32)
        masks = mask_ref[g]
        signed[pl.ds(0, half), :] = table * masks[0:1, :]
        signed[pl.ds(half, half), :] = table * masks[1:2, :]
        rows = []
        for t in range(lats):
            row = signed[pl.ds(lat_ref[t], 1), :]
            rows.append(jnp.where(same, row, 0.0))
        left = jnp.concatenate(rows, axis=0).astype(jnp.bfloat16)
        right = turned[g].astype(jnp.bfloat16)
        total = jnp.dot(left, right, preferred_element_type=jnp.float32)
        return total.reshape(lats, GROUP, pairs)

    def pair_of_groups(h, carry):
        both = jnp.concatenate([group_sum(2 * h), group_sum(2 * h + 1)], axis=1)
        start = pl.multiple_of(h * 2 * GROUP, 2 * GROUP)
        out_ref[:, pl.ds(start, 2 * GROUP), :] = both.astype(jnp.bfloat16)
        return carry

    lax.fori_loop(0, block // (2 * GROUP), pair_of_groups, 0)


def partial_sums(lat_order, slab, table, masks):
    totals, pairs, rows = slab.shape
    lats = lat_order.shape[0]
    half = table.shape[1]
    depth = totals * GROUP
    groups = BLOCK // GROUP
    return pl.pallas_call(
        partial_kernel,
        grid_spec=pltpu.PrefetchScalarGridSpec(
            num_scalar_prefetch=1,
            grid=(rows // BLOCK,),
            in_specs=[
                pl.BlockSpec((totals, pairs, BLOCK), lambda b, lat: (0, 0, b)),
                pl.BlockSpec((groups, half, depth), lambda b, lat: (b, 0, 0)),
                pl.BlockSpec((groups, 2, depth), lambda b, lat: (b, 0, 0)),
            ],
            out_specs=pl.BlockSpec((lats, BLOCK, pairs), lambda b, lat: (0, b, 0)),
            scratch_shapes=[
                pltpu.VMEM((groups, depth, pairs), jnp.float32),
                pltpu.VMEM((2 * half, depth), jnp.float32),
            ],
        ),
        out_shape=jax.ShapeDtypeStruct((lats, rows, pairs), jnp.bfloat16),
        compiler_params=pltpu.CompilerParams(vmem_limit_bytes=40 * 1024 * 1024),
        cost_estimate=pl.CostEstimate(
            flops=2 * rows * GROUP * totals * lats * pairs,
            bytes_accessed=2 * rows * pairs * (totals + lats),
            transcendentals=0,
        ),
    )(lat_order, slab, table, masks)


def reduce_partials(control, covariance, legendre, wave_order, lat_order, cycle_points):
    device_count = lax.axis_size("wave") * lax.axis_size("lev")
    own_totals = control.shape[0]
    total = control.shape[1]
    own_rows = legendre.shape[0]
    half_lats = legendre.shape[2]
    flat_index = lax.axis_index(("wave", "lev"))
    total_ids = flat_index * own_totals + jnp.arange(own_totals, dtype=jnp.int32)

    table = legendre.reshape(own_rows // GROUP, GROUP, device_count, own_totals, half_lats)
    table = jnp.transpose(table, (2, 0, 4, 3, 1)).reshape(
        device_count, own_rows // GROUP, half_lats, own_totals * GROUP
    )
    table = lax.all_to_all(table, ("wave", "lev"), split_axis=0, concat_axis=0, tiled=True)
    table = table.reshape(total // GROUP, half_lats, own_totals * GROUP)

    orders = wave_order.reshape(total // GROUP, 1, GROUP)
    usable = total_ids[None, :, None] >= orders
    sign = jnp.where((total_ids[None, :, None] + orders) % 2 == 1, -1.0, 1.0)
    masks = jnp.stack([jnp.where(usable, 1.0, 0.0), jnp.where(usable, sign, 0.0)], axis=1)
    masks = masks.reshape(total // GROUP, 2, own_totals * GROUP).astype(jnp.float32)

    produced = jnp.einsum("nrcl,nsl->ncsr", control, covariance, preferred_element_type=jnp.float32)
    slab = produced.astype(jnp.bfloat16)
    slab_levels = slab.shape[2]
    slab = slab.reshape(own_totals, 2 * slab_levels, total)
    partial = partial_sums(lat_order, slab, table, masks)
    coeffs = lax.psum_scatter(partial, ("wave", "lev"), scatter_dimension=0, tiled=True)[0]
    latitude = jnp.take(lat_order, flat_index)
    return fourier(coeffs, latitude, wave_order, cycle_points, half_lats, slab_levels)


def fourier(coeffs, latitude, wave_order, cycle_points, half_lats, slab_levels):
    factor = jnp.where(wave_order == 0, 1.0, 2.0).astype(jnp.float32)
    points = jnp.take(cycle_points, latitude % half_lats)
    cos_part, sin_part = trig_tables(wave_order, points, factor, LONW)
    real = coeffs[:, :slab_levels]
    imag = jnp.where((wave_order > 0)[:, None], coeffs[:, slab_levels:], 0)
    stacked = jnp.concatenate([real, imag], axis=0)
    trig_table = jnp.concatenate([cos_part, sin_part], axis=0)
    result = jnp.einsum("ks,kj->sj", stacked, trig_table, preferred_element_type=jnp.float32)
    return result.astype(jnp.bfloat16)[None]


def shards(*arrays):
    control, legendre, lat_order = arrays[0], arrays[2], arrays[4]
    own_totals, total = control.shape[:2]
    devices = lax.axis_size("wave") * lax.axis_size("lev")
    smaller = 2 * legendre.shape[2] < own_totals
    fits = total % BLOCK == 0 and legendre.shape[0] % GROUP == 0 and lat_order.shape[0] == devices
    if smaller and fits:
        return reduce_partials(*arrays)
    return exchange_slab(*arrays)


def solution(mesh):
    return jax.shard_map(
        shards,
        mesh=mesh,
        in_specs=(
            P(("wave", "lev"), None, None, None),
            P(("wave", "lev"), None, None),
            P(("wave", "lev"), None, None),
            P(),
            P(),
            P(),
        ),
        out_specs=P(("wave", "lev"), None, None),
        check_vma=False,
    )
```

```python
import jax
import jax.numpy as jnp
import numpy as np
from jax import lax
from jax.experimental import pallas as pl
from jax.experimental.pallas import tpu as pltpu
from jax.sharding import PartitionSpec as P

LONW = 2048


def trig_tables(orders, points, factor, width):
    coarse = jnp.arange(width // 64, dtype=jnp.int32) * 64
    fine = jnp.arange(64, dtype=jnp.int32)
    scale = 2.0 * jnp.pi / points.astype(jnp.float32)
    coarse_angle = (orders[:, None] * coarse[None, :] % points).astype(jnp.float32) * scale
    fine_angle = (orders[:, None] * fine[None, :] % points).astype(jnp.float32) * scale
    cos_c = jnp.cos(coarse_angle)[:, :, None]
    sin_c = jnp.sin(coarse_angle)[:, :, None]
    cos_f = jnp.cos(fine_angle)[:, None, :]
    sin_f = jnp.sin(fine_angle)[:, None, :]
    cosine = (cos_c * cos_f - sin_c * sin_f).reshape(orders.shape[0], width)
    sine = (sin_c * cos_f + cos_c * sin_f).reshape(orders.shape[0], width)
    cos_part = (factor[:, None] * cosine).astype(jnp.bfloat16)
    sin_part = (-factor[:, None] * sine).astype(jnp.bfloat16)
    return (cos_part, sin_part)


def exchange_slab(control, covariance, legendre, wave_order, lat_order, cycle_points):
    wave_count = lax.axis_size("wave")
    level_count = lax.axis_size("lev")
    own_totals = control.shape[0]
    total = control.shape[1]
    own_rows = legendre.shape[0]
    half_lats = legendre.shape[2]
    all_lats = lat_order.shape[0]
    own_lats = all_lats // (wave_count * level_count)
    flat_index = lax.axis_index(("wave", "lev"))
    total_ids = flat_index * own_totals + jnp.arange(own_totals, dtype=jnp.int32)
    usable = total_ids[:, None] >= wave_order[None, :]
    imag_usable = usable & (wave_order > 0)[None, :]
    weights = jnp.stack([usable, imag_usable], axis=2).astype(jnp.float32)
    produced = jnp.einsum("nrcl,nsl->nrcs", control, covariance, preferred_element_type=jnp.float32)
    slab = (produced * weights[:, :, :, None]).astype(jnp.bfloat16)
    slab_levels = slab.shape[3]
    moved = lax.all_to_all(
        lax.all_to_all(slab, "wave", split_axis=1, concat_axis=0, tiled=True),
        "lev",
        split_axis=1,
        concat_axis=0,
        tiled=True,
    )
    moved = moved.reshape(level_count, wave_count, own_totals, own_rows, 2, slab_levels)
    moved = jnp.transpose(moved, (1, 0, 2, 3, 4, 5)).reshape(total, own_rows, 2, slab_levels)
    own_orders = lax.dynamic_slice_in_dim(wave_order, flat_index * own_rows, own_rows, 0)
    odd_order = own_orders % 2 == 1
    paired = moved.reshape(total // 2, 2, own_rows, 2, slab_levels)
    pick_moved = odd_order[None, :, None, None]
    even_moved = jnp.where(pick_moved, paired[:, 1], paired[:, 0])
    odd_moved = jnp.where(pick_moved, paired[:, 0], paired[:, 1])
    table_pairs = legendre.reshape(own_rows, total // 2, 2, half_lats)
    pick_table = odd_order[:, None, None]
    even_table = jnp.where(pick_table, table_pairs[:, :, 1], table_pairs[:, :, 0])
    odd_table = jnp.where(pick_table, table_pairs[:, :, 0], table_pairs[:, :, 1])
    even_sum = jnp.einsum(
        "rqk,qrcs->rkcs", even_table, even_moved, preferred_element_type=jnp.float32
    )
    odd_sum = jnp.einsum("rqk,qrcs->rkcs", odd_table, odd_moved, preferred_element_type=jnp.float32)
    coeffs = jnp.concatenate([even_sum + odd_sum, even_sum - odd_sum], axis=1).astype(jnp.bfloat16)
    ordered = jnp.take(coeffs, lat_order, axis=1)
    arrived = lax.all_to_all(
        lax.all_to_all(ordered, "wave", split_axis=1, concat_axis=0, tiled=True),
        "lev",
        split_axis=1,
        concat_axis=0,
        tiled=True,
    )
    wave_list = (
        wave_order.reshape(wave_count, level_count, own_rows).transpose(1, 0, 2).reshape(total)
    )
    row_ids = flat_index * own_lats + jnp.arange(own_lats, dtype=jnp.int32)
    latitudes = jnp.take(lat_order, row_ids)
    by_latitude = jnp.moveaxis(arrived, 1, 0)
    factor = jnp.where(wave_list == 0, 1.0, 2.0).astype(jnp.float32)

    def grid_row(pieces):
        picked, latitude = pieces
        points = jnp.take(cycle_points, latitude % half_lats)
        cos_part, sin_part = trig_tables(wave_list, points, factor, LONW)
        trig_table = jnp.concatenate([cos_part, sin_part], axis=0)
        stacked = jnp.concatenate([picked[:, 0, :], picked[:, 1, :]], axis=0)
        result = jnp.einsum("ks,kj->sj", stacked, trig_table, preferred_element_type=jnp.float32)
        return result.astype(jnp.bfloat16)

    return lax.map(grid_row, (by_latitude, latitudes))


GROUP = 8
BLOCK = 128


def fused_kernel(
    pick_ref, slab_ref, table_ref, mask_ref, out_ref,
    turned, picked, part, from_core, from_first, from_second, from_z, send_sem, recv_sem,
):
    totals, pairs, block = slab_ref.shape
    groups, half, depth = table_ref.shape
    lats = pick_ref.shape[1]
    blocks, z_count = part.shape[0], part.shape[4]
    step = pl.program_id(0)
    wave, y = lax.axis_index("wave"), lax.axis_index("lev")
    core, x, z = wave % 2, (wave // 2) % 2, wave // 4

    def z_other(k):
        return lax.rem(z + k, z_count)

    def hop(b, stage):
        odd = b % 2
        first = x + odd * (y - x)
        second = y + odd * (x - y)
        if stage == 0:
            source, target = part.at[b, 1 - core], from_core.at[b]
            device = (wave + 1 - 2 * core, y)
        elif stage == 1:
            source, target = part.at[b, core, 1 - first], from_first.at[b]
            device = (wave + (1 - odd) * (2 - 4 * x), y + odd * (1 - 2 * y))
        elif stage == 2:
            source, target = part.at[b, core, first, 1 - second], from_second.at[b]
            device = (wave + odd * (2 - 4 * x), y + (1 - odd) * (1 - 2 * y))
        else:
            k = stage - 2
            source, target = part.at[b, core, first, second, z_other(k)], from_z.at[b, k - 1]
            device = (z_other(k) * 4 + x * 2 + core, y)
        return pltpu.make_async_remote_copy(
            src_ref=source,
            dst_ref=target,
            send_sem=send_sem.at[b, stage],
            recv_sem=recv_sem.at[b, stage],
            device_id=device,
            device_id_type=pl.DeviceIdType.MESH,
        )

    @pl.when(step == 0)
    def _():
        barrier = pltpu.get_barrier_semaphore()
        partners = [(wave + 1 - 2 * core, y), (wave + 2 - 4 * x, y), (wave, 1 - y)]
        partners += [(z_other(k) * 4 + x * 2 + core, y) for k in range(1, z_count)]
        for partner in partners:
            pl.semaphore_signal(
                barrier, inc=1, device_id=partner, device_id_type=pl.DeviceIdType.MESH
            )
        pl.semaphore_wait(barrier, len(partners))

    @pl.when(step < blocks)
    def _():
        def turn(n, carry):
            flipped = slab_ref[n].astype(jnp.float32).T
            start = pl.multiple_of(n * GROUP, GROUP)
            turned[:, pl.ds(start, GROUP), :] = flipped.reshape(groups, GROUP, pairs)
            return carry

        lax.fori_loop(0, totals, turn, 0, unroll=4)
        same = lax.broadcasted_iota(jnp.int32, (GROUP, depth), 1) % GROUP == lax.broadcasted_iota(
            jnp.int32, (GROUP, depth), 0
        )
        pick = pick_ref[step % 2]

        def group_sum(g, slot):
            table = table_ref[g].astype(jnp.float32)
            masks = mask_ref[g]
            both = jnp.concatenate([table * masks[0:1, :], table * masks[1:2, :]], axis=0)
            picked[slot] = jnp.dot(
                pick, both.astype(jnp.bfloat16), preferred_element_type=jnp.float32
            )
            rows = []
            for t in range(lats):
                rows.append(jnp.where(same, picked[slot, t : t + 1, :], 0.0))
            left = jnp.concatenate(rows, axis=0).astype(jnp.bfloat16)
            right = turned[g].astype(jnp.bfloat16)
            total = jnp.dot(left, right, preferred_element_type=jnp.float32)
            return total.reshape(lats, GROUP, pairs)

        def pair_of_groups(h, carry):
            both = jnp.concatenate([group_sum(2 * h, 0), group_sum(2 * h + 1, 1)], axis=1)
            both = both.astype(jnp.bfloat16).reshape(2, 2, 2, z_count, 2 * GROUP, pairs)
            start = pl.multiple_of(h * 2 * GROUP, 2 * GROUP)
            part[step, :, :, :, :, pl.ds(start, 2 * GROUP), :] = both
            return carry

        lax.fori_loop(0, groups // 2, pair_of_groups, 0)
        hop(step, 0).start()

    def add(to, arrived):
        return (to.astype(jnp.float32) + arrived.astype(jnp.float32)).astype(jnp.bfloat16)

    @pl.when((step >= 1) & (step < blocks + 1))
    def _():
        b = step - 1
        hop(b, 0).wait()

        def slab_add(i, carry):
            part[b, core, i // 2, i % 2] = add(
                part[b, core, i // 2, i % 2], from_core[b, i // 2, i % 2]
            )
            return carry

        lax.fori_loop(0, 4, slab_add, 0)
        hop(b, 1).start()

    @pl.when((step >= 2) & (step < blocks + 2))
    def _():
        b = step - 2
        first = x + (b % 2) * (y - x)
        hop(b, 1).wait()

        def slab_add(i, carry):
            part[b, core, first, i] = add(part[b, core, first, i], from_first[b, i])
            return carry

        lax.fori_loop(0, 2, slab_add, 0)
        hop(b, 2).start()

    @pl.when((step >= 3) & (step < blocks + 3))
    def _():
        b = step - 3
        first = x + (b % 2) * (y - x)
        second = y + (b % 2) * (x - y)
        hop(b, 2).wait()
        part[b, core, first, second] = add(part[b, core, first, second], from_second[b])
        for k in range(1, z_count):
            hop(b, 2 + k).start()

    @pl.when(step >= 4)
    def _():
        b = step - 4
        first = x + (b % 2) * (y - x)
        second = y + (b % 2) * (x - y)
        total = part[b, core, first, second, z].astype(jnp.float32)
        for k in range(1, z_count):
            hop(b, 2 + k).wait()
            total = total + from_z[b, k - 1].astype(jnp.float32)
        start = pl.multiple_of(b * block, block)
        out_ref[pl.ds(start, block), :] = total.astype(jnp.bfloat16)


def reduced_sums(pick, slab, table, masks, z_count):
    totals, pairs, rows = slab.shape
    lats = pick.shape[1]
    half = table.shape[1]
    depth = totals * GROUP
    groups = BLOCK // GROUP
    blocks = rows // BLOCK
    last = blocks - 1
    tile = (BLOCK, pairs)
    stages = 3 + z_count - 1
    return pl.pallas_call(
        fused_kernel,
        grid=(blocks + 4,),
        in_specs=[
            pl.BlockSpec((2, lats, 2 * half), lambda b: (0, 0, 0)),
            pl.BlockSpec((totals, pairs, BLOCK), lambda b: (0, 0, jnp.minimum(b, last))),
            pl.BlockSpec((groups, half, depth), lambda b: (jnp.minimum(b, last), 0, 0)),
            pl.BlockSpec((groups, 2, depth), lambda b: (jnp.minimum(b, last), 0, 0)),
        ],
        out_specs=pl.BlockSpec((rows, pairs), lambda b: (0, 0)),
        scratch_shapes=[
            pltpu.VMEM((groups, depth, pairs), jnp.float32),
            pltpu.VMEM((2, lats, depth), jnp.float32),
            pltpu.VMEM((blocks, 2, 2, 2, z_count) + tile, jnp.bfloat16),
            pltpu.VMEM((blocks, 2, 2, z_count) + tile, jnp.bfloat16),
            pltpu.VMEM((blocks, 2, z_count) + tile, jnp.bfloat16),
            pltpu.VMEM((blocks, z_count) + tile, jnp.bfloat16),
            pltpu.VMEM((blocks, z_count - 1) + tile, jnp.bfloat16),
            pltpu.SemaphoreType.DMA((blocks, stages)),
            pltpu.SemaphoreType.DMA((blocks, stages)),
        ],
        out_shape=jax.ShapeDtypeStruct((rows, pairs), jnp.bfloat16),
        compiler_params=pltpu.CompilerParams(
            vmem_limit_bytes=44 * 1024 * 1024, collective_id=0, has_side_effects=True
        ),
        cost_estimate=pl.CostEstimate(
            flops=2 * rows * GROUP * totals * lats * pairs,
            bytes_accessed=2 * rows * pairs * totals,
            transcendentals=0,
        ),
    )(pick, slab, table, masks)


def reduce_partials(control, covariance, legendre, wave_order, lat_order, cycle_points):
    device_count = lax.axis_size("wave") * lax.axis_size("lev")
    own_totals = control.shape[0]
    total = control.shape[1]
    own_rows = legendre.shape[0]
    half_lats = legendre.shape[2]
    flat_index = lax.axis_index(("wave", "lev"))
    total_ids = flat_index * own_totals + jnp.arange(own_totals, dtype=jnp.int32)

    table = legendre.reshape(own_rows // GROUP, GROUP, device_count, own_totals, half_lats)
    table = jnp.transpose(table, (2, 0, 4, 3, 1)).reshape(
        device_count, own_rows // GROUP, half_lats, own_totals * GROUP
    )
    table = lax.all_to_all(table, ("wave", "lev"), split_axis=0, concat_axis=0, tiled=True)
    table = table.reshape(total // GROUP, half_lats, own_totals * GROUP)

    orders = wave_order.reshape(total // GROUP, 1, GROUP)
    usable = total_ids[None, :, None] >= orders
    sign = jnp.where((total_ids[None, :, None] + orders) % 2 == 1, -1.0, 1.0)
    masks = jnp.stack([jnp.where(usable, 1.0, 0.0), jnp.where(usable, sign, 0.0)], axis=1)
    masks = masks.reshape(total // GROUP, 2, own_totals * GROUP).astype(jnp.float32)

    produced = jnp.einsum("nrcl,nsl->ncsr", control, covariance, preferred_element_type=jnp.float32)
    slab = produced.astype(jnp.bfloat16)
    slab_levels = slab.shape[2]
    slab = slab.reshape(own_totals, 2 * slab_levels, total)
    z_count = lax.axis_size("wave") // 4
    owner = np.arange(device_count).reshape(z_count, 2, 2, 2)
    owners = np.stack(
        [owner.transpose(2, 1, 3, 0).reshape(-1), owner.transpose(2, 3, 1, 0).reshape(-1)]
    )
    wanted = lat_order[owners][:, :, None] == jnp.arange(2 * half_lats, dtype=jnp.int32)
    pick = wanted.astype(jnp.bfloat16)
    coeffs = reduced_sums(pick, slab, table, masks, z_count)
    latitude = jnp.take(lat_order, flat_index)
    return fourier(coeffs, latitude, wave_order, cycle_points, half_lats, slab_levels)


def fourier(coeffs, latitude, wave_order, cycle_points, half_lats, slab_levels):
    factor = jnp.where(wave_order == 0, 1.0, 2.0).astype(jnp.float32)
    points = jnp.take(cycle_points, latitude % half_lats)
    cos_part, sin_part = trig_tables(wave_order, points, factor, LONW)
    real = coeffs[:, :slab_levels]
    imag = jnp.where((wave_order > 0)[:, None], coeffs[:, slab_levels:], 0)
    stacked = jnp.concatenate([real, imag], axis=0)
    trig_table = jnp.concatenate([cos_part, sin_part], axis=0)
    result = jnp.einsum("ks,kj->sj", stacked, trig_table, preferred_element_type=jnp.float32)
    return result.astype(jnp.bfloat16)[None]


def shards(*arrays):
    control, legendre, lat_order = arrays[0], arrays[2], arrays[4]
    own_totals, total = control.shape[:2]
    devices = lax.axis_size("wave") * lax.axis_size("lev")
    smaller = 2 * legendre.shape[2] < own_totals
    fits = total % BLOCK == 0 and legendre.shape[0] % GROUP == 0 and lat_order.shape[0] == devices
    fits = fits and lax.axis_size("lev") == 2 and lax.axis_size("wave") % 4 == 0
    if smaller and fits:
        return reduce_partials(*arrays)
    return exchange_slab(*arrays)


def solution(mesh):
    return jax.shard_map(
        shards,
        mesh=mesh,
        in_specs=(
            P(("wave", "lev"), None, None, None),
            P(("wave", "lev"), None, None),
            P(("wave", "lev"), None, None),
            P(),
            P(),
            P(),
        ),
        out_specs=P(("wave", "lev"), None, None),
        check_vma=False,
    )
```

```python
import jax
import jax.numpy as jnp
import numpy as np
from jax import lax
from jax.experimental import pallas as pl
from jax.experimental.pallas import tpu as pltpu
from jax.sharding import PartitionSpec as P

LONW = 2048


def trig_tables(orders, points, factor, width):
    coarse = jnp.arange(width // 64, dtype=jnp.int32) * 64
    fine = jnp.arange(64, dtype=jnp.int32)
    scale = 2.0 * jnp.pi / points.astype(jnp.float32)
    coarse_angle = (orders[:, None] * coarse[None, :] % points).astype(jnp.float32) * scale
    fine_angle = (orders[:, None] * fine[None, :] % points).astype(jnp.float32) * scale
    cos_c = jnp.cos(coarse_angle)[:, :, None]
    sin_c = jnp.sin(coarse_angle)[:, :, None]
    cos_f = jnp.cos(fine_angle)[:, None, :]
    sin_f = jnp.sin(fine_angle)[:, None, :]
    cosine = (cos_c * cos_f - sin_c * sin_f).reshape(orders.shape[0], width)
    sine = (sin_c * cos_f + cos_c * sin_f).reshape(orders.shape[0], width)
    cos_part = (factor[:, None] * cosine).astype(jnp.bfloat16)
    sin_part = (-factor[:, None] * sine).astype(jnp.bfloat16)
    return (cos_part, sin_part)


def exchange_slab(control, covariance, legendre, wave_order, lat_order, cycle_points):
    wave_count = lax.axis_size("wave")
    level_count = lax.axis_size("lev")
    own_totals = control.shape[0]
    total = control.shape[1]
    own_rows = legendre.shape[0]
    half_lats = legendre.shape[2]
    all_lats = lat_order.shape[0]
    own_lats = all_lats // (wave_count * level_count)
    flat_index = lax.axis_index(("wave", "lev"))
    total_ids = flat_index * own_totals + jnp.arange(own_totals, dtype=jnp.int32)
    usable = total_ids[:, None] >= wave_order[None, :]
    imag_usable = usable & (wave_order > 0)[None, :]
    weights = jnp.stack([usable, imag_usable], axis=2).astype(jnp.float32)
    produced = jnp.einsum("nrcl,nsl->nrcs", control, covariance, preferred_element_type=jnp.float32)
    slab = (produced * weights[:, :, :, None]).astype(jnp.bfloat16)
    slab_levels = slab.shape[3]
    moved = lax.all_to_all(
        lax.all_to_all(slab, "wave", split_axis=1, concat_axis=0, tiled=True),
        "lev",
        split_axis=1,
        concat_axis=0,
        tiled=True,
    )
    moved = moved.reshape(level_count, wave_count, own_totals, own_rows, 2, slab_levels)
    moved = jnp.transpose(moved, (1, 0, 2, 3, 4, 5)).reshape(total, own_rows, 2, slab_levels)
    own_orders = lax.dynamic_slice_in_dim(wave_order, flat_index * own_rows, own_rows, 0)
    odd_order = own_orders % 2 == 1
    paired = moved.reshape(total // 2, 2, own_rows, 2, slab_levels)
    pick_moved = odd_order[None, :, None, None]
    even_moved = jnp.where(pick_moved, paired[:, 1], paired[:, 0])
    odd_moved = jnp.where(pick_moved, paired[:, 0], paired[:, 1])
    table_pairs = legendre.reshape(own_rows, total // 2, 2, half_lats)
    pick_table = odd_order[:, None, None]
    even_table = jnp.where(pick_table, table_pairs[:, :, 1], table_pairs[:, :, 0])
    odd_table = jnp.where(pick_table, table_pairs[:, :, 0], table_pairs[:, :, 1])
    even_sum = jnp.einsum(
        "rqk,qrcs->rkcs", even_table, even_moved, preferred_element_type=jnp.float32
    )
    odd_sum = jnp.einsum("rqk,qrcs->rkcs", odd_table, odd_moved, preferred_element_type=jnp.float32)
    coeffs = jnp.concatenate([even_sum + odd_sum, even_sum - odd_sum], axis=1).astype(jnp.bfloat16)
    ordered = jnp.take(coeffs, lat_order, axis=1)
    arrived = lax.all_to_all(
        lax.all_to_all(ordered, "wave", split_axis=1, concat_axis=0, tiled=True),
        "lev",
        split_axis=1,
        concat_axis=0,
        tiled=True,
    )
    wave_list = (
        wave_order.reshape(wave_count, level_count, own_rows).transpose(1, 0, 2).reshape(total)
    )
    row_ids = flat_index * own_lats + jnp.arange(own_lats, dtype=jnp.int32)
    latitudes = jnp.take(lat_order, row_ids)
    by_latitude = jnp.moveaxis(arrived, 1, 0)
    factor = jnp.where(wave_list == 0, 1.0, 2.0).astype(jnp.float32)

    def grid_row(pieces):
        picked, latitude = pieces
        points = jnp.take(cycle_points, latitude % half_lats)
        cos_part, sin_part = trig_tables(wave_list, points, factor, LONW)
        trig_table = jnp.concatenate([cos_part, sin_part], axis=0)
        stacked = jnp.concatenate([picked[:, 0, :], picked[:, 1, :]], axis=0)
        result = jnp.einsum("ks,kj->sj", stacked, trig_table, preferred_element_type=jnp.float32)
        return result.astype(jnp.bfloat16)

    return lax.map(grid_row, (by_latitude, latitudes))


GROUP = 8
BLOCK = 128
LANES = 128


def spread_kernel(legendre_ref, out_ref, place):
    row_groups, group, half, totals = legendre_ref.shape
    wide = out_ref.shape[3]
    depth = group * LANES
    source = lax.broadcasted_iota(jnp.int32, (depth, depth), 0)
    target = lax.broadcasted_iota(jnp.int32, (depth, depth), 1)
    wanted = (source % LANES) * group + source // LANES
    place[...] = jnp.where(wanted == target, 1.0, 0.0).astype(jnp.bfloat16)
    for c in range(totals // LANES):
        rows = [
            legendre_ref[:, g, :, c * LANES : (c + 1) * LANES].reshape(row_groups * half, LANES)
            for g in range(group)
        ]
        left = jnp.concatenate(rows, axis=1)
        moved = jnp.dot(left, place[...], preferred_element_type=jnp.float32).astype(jnp.bfloat16)
        for q in range(group):
            lane = (c * group + q) * LANES
            piece = moved[:, q * LANES : (q + 1) * LANES].reshape(row_groups, half, LANES)
            out_ref[lane // wide, :, :, lane % wide : lane % wide + LANES] = piece


def spread(legendre, device_count):
    own_rows, half, totals = legendre.shape
    wide = totals // device_count * GROUP
    depth = GROUP * LANES
    return pl.pallas_call(
        spread_kernel,
        out_shape=jax.ShapeDtypeStruct(
            (device_count, own_rows // GROUP, half, wide), jnp.bfloat16
        ),
        in_specs=[pl.BlockSpec(memory_space=pltpu.VMEM)],
        out_specs=pl.BlockSpec(memory_space=pltpu.VMEM),
        scratch_shapes=[pltpu.VMEM((depth, depth), jnp.bfloat16)],
        compiler_params=pltpu.CompilerParams(vmem_limit_bytes=32 * 1024 * 1024),
        cost_estimate=pl.CostEstimate(
            flops=2 * own_rows * half * totals * depth,
            bytes_accessed=4 * own_rows * half * totals,
            transcendentals=0,
        ),
    )(legendre.reshape(own_rows // GROUP, GROUP, half, totals))


def fused_kernel(
    pick_ref, slab_ref, table_ref, mask_ref, out_ref,
    turned, picked, part, from_core, from_first, from_second, from_z, send_sem, recv_sem,
):
    totals, pairs, block = slab_ref.shape
    groups, half, depth = table_ref.shape
    lats = pick_ref.shape[1]
    blocks, z_count = part.shape[0], part.shape[4]
    step = pl.program_id(0)
    wave, y = lax.axis_index("wave"), lax.axis_index("lev")
    core, x, z = wave % 2, (wave // 2) % 2, wave // 4

    def z_other(k):
        return lax.rem(z + k, z_count)

    def hop(b, stage):
        odd = b % 2
        first = x + odd * (y - x)
        second = y + odd * (x - y)
        if stage == 0:
            source, target = part.at[b, 1 - core], from_core.at[b]
            device = (wave + 1 - 2 * core, y)
        elif stage == 1:
            source, target = part.at[b, core, 1 - first], from_first.at[b]
            device = (wave + (1 - odd) * (2 - 4 * x), y + odd * (1 - 2 * y))
        elif stage == 2:
            source, target = part.at[b, core, first, 1 - second], from_second.at[b]
            device = (wave + odd * (2 - 4 * x), y + (1 - odd) * (1 - 2 * y))
        else:
            k = stage - 2
            source, target = part.at[b, core, first, second, z_other(k)], from_z.at[b, k - 1]
            device = (z_other(k) * 4 + x * 2 + core, y)
        return pltpu.make_async_remote_copy(
            src_ref=source,
            dst_ref=target,
            send_sem=send_sem.at[b, stage],
            recv_sem=recv_sem.at[b, stage],
            device_id=device,
            device_id_type=pl.DeviceIdType.MESH,
        )

    @pl.when(step == 0)
    def _():
        barrier = pltpu.get_barrier_semaphore()
        partners = [(wave + 1 - 2 * core, y), (wave + 2 - 4 * x, y), (wave, 1 - y)]
        partners += [(z_other(k) * 4 + x * 2 + core, y) for k in range(1, z_count)]
        for partner in partners:
            pl.semaphore_signal(
                barrier, inc=1, device_id=partner, device_id_type=pl.DeviceIdType.MESH
            )
        pl.semaphore_wait(barrier, len(partners))

    @pl.when(step < blocks)
    def _():
        def turn(n, carry):
            flipped = slab_ref[n].astype(jnp.float32).T
            start = pl.multiple_of(n * GROUP, GROUP)
            turned[:, pl.ds(start, GROUP), :] = flipped.reshape(groups, GROUP, pairs)
            return carry

        lax.fori_loop(0, totals, turn, 0, unroll=8)
        same = lax.broadcasted_iota(jnp.int32, (GROUP, depth), 1) % GROUP == lax.broadcasted_iota(
            jnp.int32, (GROUP, depth), 0
        )
        pick = pick_ref[step % 2]

        def choose(g, carry):
            table = table_ref[g].astype(jnp.float32)
            masks = mask_ref[g]
            both = jnp.concatenate([table * masks[0:1, :], table * masks[1:2, :]], axis=0)
            picked[g] = jnp.dot(
                pick, both.astype(jnp.bfloat16), preferred_element_type=jnp.float32
            )
            return carry

        lax.fori_loop(0, groups, choose, 0, unroll=8)

        def group_sum(g):
            rows = [jnp.where(same, picked[g, t : t + 1, :], 0.0) for t in range(lats)]
            left = jnp.concatenate(rows, axis=0).astype(jnp.bfloat16)
            right = turned[g].astype(jnp.bfloat16)
            total = jnp.dot(left, right, preferred_element_type=jnp.float32)
            return total.reshape(lats, GROUP, pairs)

        def pair_of_groups(h, carry):
            both = jnp.concatenate([group_sum(2 * h), group_sum(2 * h + 1)], axis=1)
            both = both.astype(jnp.bfloat16).reshape(2, 2, 2, z_count, 2 * GROUP, pairs)
            start = pl.multiple_of(h * 2 * GROUP, 2 * GROUP)
            part[step, :, :, :, :, pl.ds(start, 2 * GROUP), :] = both
            return carry

        lax.fori_loop(0, groups // 2, pair_of_groups, 0, unroll=2)
        hop(step, 0).start()

    def add(to, arrived):
        return (to.astype(jnp.float32) + arrived.astype(jnp.float32)).astype(jnp.bfloat16)

    @pl.when((step >= 1) & (step < blocks + 1))
    def _():
        b = step - 1
        hop(b, 0).wait()

        def slab_add(i, carry):
            part[b, core, i // 2, i % 2] = add(
                part[b, core, i // 2, i % 2], from_core[b, i // 2, i % 2]
            )
            return carry

        lax.fori_loop(0, 4, slab_add, 0)
        hop(b, 1).start()

    @pl.when((step >= 2) & (step < blocks + 2))
    def _():
        b = step - 2
        first = x + (b % 2) * (y - x)
        hop(b, 1).wait()

        def slab_add(i, carry):
            part[b, core, first, i] = add(part[b, core, first, i], from_first[b, i])
            return carry

        lax.fori_loop(0, 2, slab_add, 0)
        hop(b, 2).start()

    @pl.when((step >= 3) & (step < blocks + 3))
    def _():
        b = step - 3
        first = x + (b % 2) * (y - x)
        second = y + (b % 2) * (x - y)
        hop(b, 2).wait()
        part[b, core, first, second] = add(part[b, core, first, second], from_second[b])
        for k in range(1, z_count):
            hop(b, 2 + k).start()

    @pl.when(step >= 4)
    def _():
        b = step - 4
        first = x + (b % 2) * (y - x)
        second = y + (b % 2) * (x - y)
        total = part[b, core, first, second, z].astype(jnp.float32)
        for k in range(1, z_count):
            hop(b, 2 + k).wait()
            total = total + from_z[b, k - 1].astype(jnp.float32)
        start = pl.multiple_of(b * block, block)
        out_ref[pl.ds(start, block), :] = total.astype(jnp.bfloat16)


def reduced_sums(pick, slab, table, masks, z_count):
    totals, pairs, rows = slab.shape
    lats = pick.shape[1]
    half = table.shape[1]
    depth = totals * GROUP
    groups = BLOCK // GROUP
    blocks = rows // BLOCK
    last = blocks - 1
    tile = (BLOCK, pairs)
    stages = 3 + z_count - 1
    return pl.pallas_call(
        fused_kernel,
        grid=(blocks + 4,),
        in_specs=[
            pl.BlockSpec((2, lats, 2 * half), lambda b: (0, 0, 0)),
            pl.BlockSpec((totals, pairs, BLOCK), lambda b: (0, 0, jnp.minimum(b, last))),
            pl.BlockSpec((groups, half, depth), lambda b: (jnp.minimum(b, last), 0, 0)),
            pl.BlockSpec((groups, 2, depth), lambda b: (jnp.minimum(b, last), 0, 0)),
        ],
        out_specs=pl.BlockSpec((rows, pairs), lambda b: (0, 0)),
        scratch_shapes=[
            pltpu.VMEM((groups, depth, pairs), jnp.float32),
            pltpu.VMEM((groups, lats, depth), jnp.float32),
            pltpu.VMEM((blocks, 2, 2, 2, z_count) + tile, jnp.bfloat16),
            pltpu.VMEM((blocks, 2, 2, z_count) + tile, jnp.bfloat16),
            pltpu.VMEM((blocks, 2, z_count) + tile, jnp.bfloat16),
            pltpu.VMEM((blocks, z_count) + tile, jnp.bfloat16),
            pltpu.VMEM((blocks, z_count - 1) + tile, jnp.bfloat16),
            pltpu.SemaphoreType.DMA((blocks, stages)),
            pltpu.SemaphoreType.DMA((blocks, stages)),
        ],
        out_shape=jax.ShapeDtypeStruct((rows, pairs), jnp.bfloat16),
        compiler_params=pltpu.CompilerParams(
            vmem_limit_bytes=44 * 1024 * 1024, collective_id=0, has_side_effects=True
        ),
        cost_estimate=pl.CostEstimate(
            flops=2 * rows * GROUP * totals * lats * pairs,
            bytes_accessed=2 * rows * pairs * totals,
            transcendentals=0,
        ),
    )(pick, slab, table, masks)


def reduce_partials(control, covariance, legendre, wave_order, lat_order, cycle_points):
    device_count = lax.axis_size("wave") * lax.axis_size("lev")
    own_totals = control.shape[0]
    total = control.shape[1]
    own_rows = legendre.shape[0]
    half_lats = legendre.shape[2]
    flat_index = lax.axis_index(("wave", "lev"))
    total_ids = flat_index * own_totals + jnp.arange(own_totals, dtype=jnp.int32)

    table = spread(jnp.transpose(legendre, (0, 2, 1)), device_count)
    table = lax.all_to_all(table, ("wave", "lev"), split_axis=0, concat_axis=0, tiled=True)
    table = table.reshape(total // GROUP, half_lats, own_totals * GROUP)

    orders = wave_order.reshape(total // GROUP, 1, GROUP)
    usable = total_ids[None, :, None] >= orders
    sign = jnp.where((total_ids[None, :, None] + orders) % 2 == 1, -1.0, 1.0)
    masks = jnp.stack([jnp.where(usable, 1.0, 0.0), jnp.where(usable, sign, 0.0)], axis=1)
    masks = masks.reshape(total // GROUP, 2, own_totals * GROUP).astype(jnp.float32)

    produced = jnp.einsum("nrcl,nsl->ncsr", control, covariance, preferred_element_type=jnp.float32)
    slab = produced.astype(jnp.bfloat16)
    slab_levels = slab.shape[2]
    slab = slab.reshape(own_totals, 2 * slab_levels, total)
    z_count = lax.axis_size("wave") // 4
    owner = np.arange(device_count).reshape(z_count, 2, 2, 2)
    owners = np.stack(
        [owner.transpose(2, 1, 3, 0).reshape(-1), owner.transpose(2, 3, 1, 0).reshape(-1)]
    )
    wanted = lat_order[owners][:, :, None] == jnp.arange(2 * half_lats, dtype=jnp.int32)
    pick = wanted.astype(jnp.bfloat16)
    coeffs = reduced_sums(pick, slab, table, masks, z_count)
    latitude = jnp.take(lat_order, flat_index)
    return fourier(coeffs, latitude, wave_order, cycle_points, half_lats, slab_levels)


def fourier(coeffs, latitude, wave_order, cycle_points, half_lats, slab_levels):
    factor = jnp.where(wave_order == 0, 1.0, 2.0).astype(jnp.float32)
    points = jnp.take(cycle_points, latitude % half_lats)
    cos_part, sin_part = trig_tables(wave_order, points, factor, LONW)
    real = coeffs[:, :slab_levels]
    imag = jnp.where((wave_order > 0)[:, None], coeffs[:, slab_levels:], 0)
    stacked = jnp.concatenate([real, imag], axis=0)
    trig_table = jnp.concatenate([cos_part, sin_part], axis=0)
    result = jnp.einsum("ks,kj->sj", stacked, trig_table, preferred_element_type=jnp.float32)
    return result.astype(jnp.bfloat16)[None]


def shards(*arrays):
    control, legendre, lat_order = arrays[0], arrays[2], arrays[4]
    own_totals, total = control.shape[:2]
    devices = lax.axis_size("wave") * lax.axis_size("lev")
    smaller = 2 * legendre.shape[2] < own_totals
    fits = total % BLOCK == 0 and legendre.shape[0] % GROUP == 0 and lat_order.shape[0] == devices
    fits = fits and total % LANES == 0 and total // devices * GROUP % LANES == 0
    fits = fits and lax.axis_size("lev") == 2 and lax.axis_size("wave") % 4 == 0
    if smaller and fits:
        return reduce_partials(*arrays)
    return exchange_slab(*arrays)


def solution(mesh):
    return jax.shard_map(
        shards,
        mesh=mesh,
        in_specs=(
            P(("wave", "lev"), None, None, None),
            P(("wave", "lev"), None, None),
            P(("wave", "lev"), None, None),
            P(),
            P(),
            P(),
        ),
        out_specs=P(("wave", "lev"), None, None),
        check_vma=False,
    )
```

```python
import jax
import jax.numpy as jnp
import numpy as np
from jax import lax
from jax.experimental import pallas as pl
from jax.experimental.pallas import tpu as pltpu
from jax.sharding import PartitionSpec as P

LONW = 2048


def trig_tables(orders, points, factor, width):
    coarse = jnp.arange(width // 64, dtype=jnp.int32) * 64
    fine = jnp.arange(64, dtype=jnp.int32)
    scale = 2.0 * jnp.pi / points.astype(jnp.float32)
    coarse_angle = (orders[:, None] * coarse[None, :] % points).astype(jnp.float32) * scale
    fine_angle = (orders[:, None] * fine[None, :] % points).astype(jnp.float32) * scale
    cos_c = jnp.cos(coarse_angle)[:, :, None]
    sin_c = jnp.sin(coarse_angle)[:, :, None]
    cos_f = jnp.cos(fine_angle)[:, None, :]
    sin_f = jnp.sin(fine_angle)[:, None, :]
    cosine = (cos_c * cos_f - sin_c * sin_f).reshape(orders.shape[0], width)
    sine = (sin_c * cos_f + cos_c * sin_f).reshape(orders.shape[0], width)
    cos_part = (factor[:, None] * cosine).astype(jnp.bfloat16)
    sin_part = (-factor[:, None] * sine).astype(jnp.bfloat16)
    return (cos_part, sin_part)


def exchange_slab(control, covariance, legendre, wave_order, lat_order, cycle_points):
    wave_count = lax.axis_size("wave")
    level_count = lax.axis_size("lev")
    own_totals = control.shape[0]
    total = control.shape[1]
    own_rows = legendre.shape[0]
    half_lats = legendre.shape[2]
    all_lats = lat_order.shape[0]
    own_lats = all_lats // (wave_count * level_count)
    flat_index = lax.axis_index(("wave", "lev"))
    total_ids = flat_index * own_totals + jnp.arange(own_totals, dtype=jnp.int32)
    usable = total_ids[:, None] >= wave_order[None, :]
    imag_usable = usable & (wave_order > 0)[None, :]
    weights = jnp.stack([usable, imag_usable], axis=2).astype(jnp.float32)
    produced = jnp.einsum("nrcl,nsl->nrcs", control, covariance, preferred_element_type=jnp.float32)
    slab = (produced * weights[:, :, :, None]).astype(jnp.bfloat16)
    slab_levels = slab.shape[3]
    moved = lax.all_to_all(
        lax.all_to_all(slab, "wave", split_axis=1, concat_axis=0, tiled=True),
        "lev",
        split_axis=1,
        concat_axis=0,
        tiled=True,
    )
    moved = moved.reshape(level_count, wave_count, own_totals, own_rows, 2, slab_levels)
    moved = jnp.transpose(moved, (1, 0, 2, 3, 4, 5)).reshape(total, own_rows, 2, slab_levels)
    own_orders = lax.dynamic_slice_in_dim(wave_order, flat_index * own_rows, own_rows, 0)
    odd_order = own_orders % 2 == 1
    paired = moved.reshape(total // 2, 2, own_rows, 2, slab_levels)
    pick_moved = odd_order[None, :, None, None]
    even_moved = jnp.where(pick_moved, paired[:, 1], paired[:, 0])
    odd_moved = jnp.where(pick_moved, paired[:, 0], paired[:, 1])
    table_pairs = legendre.reshape(own_rows, total // 2, 2, half_lats)
    pick_table = odd_order[:, None, None]
    even_table = jnp.where(pick_table, table_pairs[:, :, 1], table_pairs[:, :, 0])
    odd_table = jnp.where(pick_table, table_pairs[:, :, 0], table_pairs[:, :, 1])
    even_sum = jnp.einsum(
        "rqk,qrcs->rkcs", even_table, even_moved, preferred_element_type=jnp.float32
    )
    odd_sum = jnp.einsum("rqk,qrcs->rkcs", odd_table, odd_moved, preferred_element_type=jnp.float32)
    coeffs = jnp.concatenate([even_sum + odd_sum, even_sum - odd_sum], axis=1).astype(jnp.bfloat16)
    ordered = jnp.take(coeffs, lat_order, axis=1)
    arrived = lax.all_to_all(
        lax.all_to_all(ordered, "wave", split_axis=1, concat_axis=0, tiled=True),
        "lev",
        split_axis=1,
        concat_axis=0,
        tiled=True,
    )
    wave_list = (
        wave_order.reshape(wave_count, level_count, own_rows).transpose(1, 0, 2).reshape(total)
    )
    row_ids = flat_index * own_lats + jnp.arange(own_lats, dtype=jnp.int32)
    latitudes = jnp.take(lat_order, row_ids)
    by_latitude = jnp.moveaxis(arrived, 1, 0)
    factor = jnp.where(wave_list == 0, 1.0, 2.0).astype(jnp.float32)

    def grid_row(pieces):
        picked, latitude = pieces
        points = jnp.take(cycle_points, latitude % half_lats)
        cos_part, sin_part = trig_tables(wave_list, points, factor, LONW)
        trig_table = jnp.concatenate([cos_part, sin_part], axis=0)
        stacked = jnp.concatenate([picked[:, 0, :], picked[:, 1, :]], axis=0)
        result = jnp.einsum("ks,kj->sj", stacked, trig_table, preferred_element_type=jnp.float32)
        return result.astype(jnp.bfloat16)

    return lax.map(grid_row, (by_latitude, latitudes))


GROUP = 8
BLOCK = 128
LANES = 128


def spread_kernel(legendre_ref, out_ref, place):
    row_groups, group, half, totals = legendre_ref.shape
    wide = out_ref.shape[3]
    depth = group * LANES
    source = lax.broadcasted_iota(jnp.int32, (depth, depth), 0)
    target = lax.broadcasted_iota(jnp.int32, (depth, depth), 1)
    wanted = (source % LANES) * group + source // LANES
    place[...] = jnp.where(wanted == target, 1.0, 0.0).astype(jnp.bfloat16)
    for c in range(totals // LANES):
        rows = [
            legendre_ref[:, g, :, c * LANES : (c + 1) * LANES].reshape(row_groups * half, LANES)
            for g in range(group)
        ]
        left = jnp.concatenate(rows, axis=1)
        moved = jnp.dot(left, place[...], preferred_element_type=jnp.float32).astype(jnp.bfloat16)
        for q in range(group):
            lane = (c * group + q) * LANES
            piece = moved[:, q * LANES : (q + 1) * LANES].reshape(row_groups, half, LANES)
            out_ref[lane // wide, :, :, lane % wide : lane % wide + LANES] = piece


def spread(legendre, device_count):
    own_rows, half, totals = legendre.shape
    wide = totals // device_count * GROUP
    depth = GROUP * LANES
    return pl.pallas_call(
        spread_kernel,
        out_shape=jax.ShapeDtypeStruct(
            (device_count, own_rows // GROUP, half, wide), jnp.bfloat16
        ),
        in_specs=[pl.BlockSpec(memory_space=pltpu.VMEM)],
        out_specs=pl.BlockSpec(memory_space=pltpu.VMEM),
        scratch_shapes=[pltpu.VMEM((depth, depth), jnp.bfloat16)],
        compiler_params=pltpu.CompilerParams(vmem_limit_bytes=32 * 1024 * 1024),
        cost_estimate=pl.CostEstimate(
            flops=2 * own_rows * half * totals * depth,
            bytes_accessed=4 * own_rows * half * totals,
            transcendentals=0,
        ),
    )(legendre.reshape(own_rows // GROUP, GROUP, half, totals))


def fused_kernel(
    pick_ref, slab_ref, table_ref, mask_ref, out_ref,
    turned, picked, part, from_core, from_first, from_second, from_z, send_sem, recv_sem,
):
    totals, pairs, block = slab_ref.shape
    groups, half, depth = table_ref.shape
    lats = pick_ref.shape[1]
    blocks, z_count = part.shape[0], part.shape[4]
    step = pl.program_id(0)
    wave, y = lax.axis_index("wave"), lax.axis_index("lev")
    core, x, z = wave % 2, (wave // 2) % 2, wave // 4

    def z_other(k):
        return lax.rem(z + k, z_count)

    def hop(b, stage):
        odd = b % 2
        first = x + odd * (y - x)
        second = y + odd * (x - y)
        if stage == 0:
            source, target = part.at[b, 1 - core], from_core.at[b]
            device = (wave + 1 - 2 * core, y)
        elif stage == 1:
            source, target = part.at[b, core, 1 - first], from_first.at[b]
            device = (wave + (1 - odd) * (2 - 4 * x), y + odd * (1 - 2 * y))
        elif stage == 2:
            source, target = part.at[b, core, first, 1 - second], from_second.at[b]
            device = (wave + odd * (2 - 4 * x), y + (1 - odd) * (1 - 2 * y))
        else:
            k = stage - 2
            source, target = part.at[b, core, first, second, z_other(k)], from_z.at[b, k - 1]
            device = (z_other(k) * 4 + x * 2 + core, y)
        return pltpu.make_async_remote_copy(
            src_ref=source,
            dst_ref=target,
            send_sem=send_sem.at[b, stage],
            recv_sem=recv_sem.at[b, stage],
            device_id=device,
            device_id_type=pl.DeviceIdType.MESH,
        )

    @pl.when(step == 0)
    def _():
        barrier = pltpu.get_barrier_semaphore()
        partners = [(wave + 1 - 2 * core, y), (wave + 2 - 4 * x, y), (wave, 1 - y)]
        partners += [(z_other(k) * 4 + x * 2 + core, y) for k in range(1, z_count)]
        for partner in partners:
            pl.semaphore_signal(
                barrier, inc=1, device_id=partner, device_id_type=pl.DeviceIdType.MESH
            )
        pl.semaphore_wait(barrier, len(partners))

    @pl.when(step < blocks)
    def _():
        def turn(n, carry):
            flipped = slab_ref[n].astype(jnp.float32).T
            start = pl.multiple_of(n * GROUP, GROUP)
            turned[:, pl.ds(start, GROUP), :] = flipped.reshape(groups, GROUP, pairs)
            return carry

        lax.fori_loop(0, totals, turn, 0, unroll=16)
        same = lax.broadcasted_iota(jnp.int32, (GROUP, depth), 1) % GROUP == lax.broadcasted_iota(
            jnp.int32, (GROUP, depth), 0
        )
        pick = pick_ref[step % 2]

        def choose(g, carry):
            table = table_ref[g].astype(jnp.float32)
            masks = mask_ref[g]
            both = jnp.concatenate([table * masks[0:1, :], table * masks[1:2, :]], axis=0)
            picked[g] = jnp.dot(
                pick, both.astype(jnp.bfloat16), preferred_element_type=jnp.float32
            )
            return carry

        lax.fori_loop(0, groups, choose, 0, unroll=16)

        def group_sum(g):
            rows = [jnp.where(same, picked[g, t : t + 1, :], 0.0) for t in range(lats)]
            left = jnp.concatenate(rows, axis=0).astype(jnp.bfloat16)
            right = turned[g].astype(jnp.bfloat16)
            total = jnp.dot(left, right, preferred_element_type=jnp.float32)
            return total.reshape(lats, GROUP, pairs)

        def pair_of_groups(h, carry):
            both = jnp.concatenate([group_sum(2 * h), group_sum(2 * h + 1)], axis=1)
            both = both.astype(jnp.bfloat16).reshape(2, 2, 2, z_count, 2 * GROUP, pairs)
            start = pl.multiple_of(h * 2 * GROUP, 2 * GROUP)
            part[step, :, :, :, :, pl.ds(start, 2 * GROUP), :] = both
            return carry

        lax.fori_loop(0, groups // 2, pair_of_groups, 0, unroll=4)
        hop(step, 0).start()

    def add(to, arrived):
        return (to.astype(jnp.float32) + arrived.astype(jnp.float32)).astype(jnp.bfloat16)

    @pl.when((step >= 1) & (step < blocks + 1))
    def _():
        b = step - 1
        hop(b, 0).wait()

        def slab_add(i, carry):
            part[b, core, i // 2, i % 2] = add(
                part[b, core, i // 2, i % 2], from_core[b, i // 2, i % 2]
            )
            return carry

        lax.fori_loop(0, 4, slab_add, 0)
        hop(b, 1).start()

    @pl.when((step >= 2) & (step < blocks + 2))
    def _():
        b = step - 2
        first = x + (b % 2) * (y - x)
        hop(b, 1).wait()

        def slab_add(i, carry):
            part[b, core, first, i] = add(part[b, core, first, i], from_first[b, i])
            return carry

        lax.fori_loop(0, 2, slab_add, 0)
        hop(b, 2).start()

    @pl.when((step >= 3) & (step < blocks + 3))
    def _():
        b = step - 3
        first = x + (b % 2) * (y - x)
        second = y + (b % 2) * (x - y)
        hop(b, 2).wait()
        part[b, core, first, second] = add(part[b, core, first, second], from_second[b])
        for k in range(1, z_count):
            hop(b, 2 + k).start()

    @pl.when(step >= 4)
    def _():
        b = step - 4
        first = x + (b % 2) * (y - x)
        second = y + (b % 2) * (x - y)
        total = part[b, core, first, second, z].astype(jnp.float32)
        for k in range(1, z_count):
            hop(b, 2 + k).wait()
            total = total + from_z[b, k - 1].astype(jnp.float32)
        start = pl.multiple_of(b * block, block)
        out_ref[pl.ds(start, block), :] = total.astype(jnp.bfloat16)


def reduced_sums(pick, slab, table, masks, z_count):
    totals, pairs, rows = slab.shape
    lats = pick.shape[1]
    half = table.shape[1]
    depth = totals * GROUP
    groups = BLOCK // GROUP
    blocks = rows // BLOCK
    last = blocks - 1
    tile = (BLOCK, pairs)
    stages = 3 + z_count - 1
    return pl.pallas_call(
        fused_kernel,
        grid=(blocks + 4,),
        in_specs=[
            pl.BlockSpec((2, lats, 2 * half), lambda b: (0, 0, 0)),
            pl.BlockSpec((totals, pairs, BLOCK), lambda b: (0, 0, jnp.minimum(b, last))),
            pl.BlockSpec((groups, half, depth), lambda b: (jnp.minimum(b, last), 0, 0)),
            pl.BlockSpec((groups, 2, depth), lambda b: (jnp.minimum(b, last), 0, 0)),
        ],
        out_specs=pl.BlockSpec((rows, pairs), lambda b: (0, 0)),
        scratch_shapes=[
            pltpu.VMEM((groups, depth, pairs), jnp.float32),
            pltpu.VMEM((groups, lats, depth), jnp.float32),
            pltpu.VMEM((blocks, 2, 2, 2, z_count) + tile, jnp.bfloat16),
            pltpu.VMEM((blocks, 2, 2, z_count) + tile, jnp.bfloat16),
            pltpu.VMEM((blocks, 2, z_count) + tile, jnp.bfloat16),
            pltpu.VMEM((blocks, z_count) + tile, jnp.bfloat16),
            pltpu.VMEM((blocks, z_count - 1) + tile, jnp.bfloat16),
            pltpu.SemaphoreType.DMA((blocks, stages)),
            pltpu.SemaphoreType.DMA((blocks, stages)),
        ],
        out_shape=jax.ShapeDtypeStruct((rows, pairs), jnp.bfloat16),
        compiler_params=pltpu.CompilerParams(
            vmem_limit_bytes=44 * 1024 * 1024, collective_id=0, has_side_effects=True
        ),
        cost_estimate=pl.CostEstimate(
            flops=2 * rows * GROUP * totals * lats * pairs,
            bytes_accessed=2 * rows * pairs * totals,
            transcendentals=0,
        ),
    )(pick, slab, table, masks)


def reduce_partials(control, covariance, legendre, wave_order, lat_order, cycle_points):
    device_count = lax.axis_size("wave") * lax.axis_size("lev")
    own_totals = control.shape[0]
    total = control.shape[1]
    own_rows = legendre.shape[0]
    half_lats = legendre.shape[2]
    flat_index = lax.axis_index(("wave", "lev"))
    total_ids = flat_index * own_totals + jnp.arange(own_totals, dtype=jnp.int32)

    table = spread(jnp.transpose(legendre, (0, 2, 1)), device_count)
    table = lax.all_to_all(table, ("wave", "lev"), split_axis=0, concat_axis=0, tiled=True)
    table = table.reshape(total // GROUP, half_lats, own_totals * GROUP)

    orders = wave_order.reshape(total // GROUP, 1, GROUP)
    usable = total_ids[None, :, None] >= orders
    sign = jnp.where((total_ids[None, :, None] + orders) % 2 == 1, -1.0, 1.0)
    masks = jnp.stack([jnp.where(usable, 1.0, 0.0), jnp.where(usable, sign, 0.0)], axis=1)
    masks = masks.reshape(total // GROUP, 2, own_totals * GROUP).astype(jnp.float32)

    produced = jnp.einsum("nrcl,nsl->ncsr", control, covariance, preferred_element_type=jnp.float32)
    slab = produced.astype(jnp.bfloat16)
    slab_levels = slab.shape[2]
    slab = slab.reshape(own_totals, 2 * slab_levels, total)
    z_count = lax.axis_size("wave") // 4
    owner = np.arange(device_count).reshape(z_count, 2, 2, 2)
    owners = np.stack(
        [owner.transpose(2, 1, 3, 0).reshape(-1), owner.transpose(2, 3, 1, 0).reshape(-1)]
    )
    wanted = lat_order[owners][:, :, None] == jnp.arange(2 * half_lats, dtype=jnp.int32)
    pick = wanted.astype(jnp.bfloat16)
    coeffs = reduced_sums(pick, slab, table, masks, z_count)
    latitude = jnp.take(lat_order, flat_index)
    return fourier(coeffs, latitude, wave_order, cycle_points, half_lats, slab_levels)


def fourier(coeffs, latitude, wave_order, cycle_points, half_lats, slab_levels):
    factor = jnp.where(wave_order == 0, 1.0, 2.0).astype(jnp.float32)
    points = jnp.take(cycle_points, latitude % half_lats)
    cos_part, sin_part = trig_tables(wave_order, points, factor, LONW)
    real = coeffs[:, :slab_levels]
    imag = jnp.where((wave_order > 0)[:, None], coeffs[:, slab_levels:], 0)
    stacked = jnp.concatenate([real, imag], axis=0)
    trig_table = jnp.concatenate([cos_part, sin_part], axis=0)
    result = jnp.einsum("ks,kj->sj", stacked, trig_table, preferred_element_type=jnp.float32)
    return result.astype(jnp.bfloat16)[None]


def shards(*arrays):
    control, legendre, lat_order = arrays[0], arrays[2], arrays[4]
    own_totals, total = control.shape[:2]
    devices = lax.axis_size("wave") * lax.axis_size("lev")
    smaller = 2 * legendre.shape[2] < own_totals
    fits = total % BLOCK == 0 and legendre.shape[0] % GROUP == 0 and lat_order.shape[0] == devices
    fits = fits and total % LANES == 0 and total // devices * GROUP % LANES == 0
    fits = fits and lax.axis_size("lev") == 2 and lax.axis_size("wave") % 4 == 0
    if smaller and fits:
        return reduce_partials(*arrays)
    return exchange_slab(*arrays)


def solution(mesh):
    return jax.shard_map(
        shards,
        mesh=mesh,
        in_specs=(
            P(("wave", "lev"), None, None, None),
            P(("wave", "lev"), None, None),
            P(("wave", "lev"), None, None),
            P(),
            P(),
            P(),
        ),
        out_specs=P(("wave", "lev"), None, None),
        check_vma=False,
    )
```
